256 devices in a mesh: section: 8 (over z), expert: 8 (over x, core), dp: 4 (over y).
Axes of the slice: x: 4, y: 4, z: 8, core: 2. Of those that a mesh axis runs over, the one named last changes fastest.
Arguments:
- in_flight: bfloat16 [2, 8, 1024, 1536], P(None, 'section', ('expert', 'dp')), may hold values from -6 to 6
- entering: bfloat16 [1, 1024, 1536], P(None, ('expert', 'dp')), may hold values from -6 to 6
- checkpoints: bfloat16 [2, 2, 8, 1024, 1536], P(None, None, 'section', ('expert', 'dp')), may hold values from -6 to 6
- expert_ids: int32 [2, 2, 8, 1024, 2], P(None, None, 'section', ('expert', 'dp')), may hold values from 0 to 7, all different within a row; in each aligned block of 32 rows (0 to 31, 32 to 63, ..., all dimensions but the last counted through in order) at most 9 rows name the same one
- gates: float32 [2, 2, 8, 1024, 2], P(None, None, 'section', ('expert', 'dp')), may hold values from 0.1 to 1
- w_in: bfloat16 [2, 8, 8, 1536, 1536], P(None, 'section', 'expert', None, 'dp'), may hold values from -0.15625 to 0.15625
- w_out: bfloat16 [2, 8, 8, 1536, 1536], P(None, 'section', 'expert', 'dp'), may hold values from -0.15625 to 0.15625
Outputs:
- out_grads: bfloat16 [2, 2, 8, 1024, 1536], P(None, None, 'section', ('expert', 'dp'))
- w_in_grad: bfloat16 [2, 8, 8, 1536, 1536], P(None, 'section', 'expert', None, 'dp')
- w_out_grad: bfloat16 [2, 8, 8, 1536, 1536], P(None, 'section', 'expert', 'dp')
The draws below stay inside these ranges and needn't reach their ends.
Inputs may be any that keep to these rules, and one draw needn't show every extreme that they name: `expert_ids`: in every tick, layer index and section, the 32 tokens of one device name each expert at most 9 times, a bound that some block reaches; the 2 experts of a token differ.
All inputs are finite; a program needn't handle non-finite values.
Results may differ from the reference program's by a relative error of at most 0.009.
Values may be sent and summed in bfloat16 or wider, within the bound.
A program may use at most 128 MiB of HBM per device.

```python
import math
import jax
import jax.numpy as jnp
import numpy as np
from jax import lax

D = 1536
FF = 1536
TOP = 2
TICKS = 2
TOK_DEV = 32
EXPERTS = 8
CAP = 9
TOKENS = 1024
N_SECTION = 8
N_DP = 4


def block_levels(rng, shape, shards, low, largest):
    def one(position, blocks):
        draws = jax.random.uniform(jax.random.fold_in(jax.random.fold_in(rng, 6), position), (blocks,), jnp.float32, low / len(shards), largest / len(shards))
        return jnp.repeat(jnp.exp(draws), shape[position] // blocks).reshape((-1,) + (1,) * (len(shape) - position - 1))

    gain = one(*shards[0])
    for cut in shards[1:]:
        gain = gain * one(*cut)
    return gain


def shared_out(rng, own, number, rows, amount, top, limit, lean):
    sequence = jax.random.permutation(rng, amount)
    crowded, ordinary = portions_of(amount, rows * top, limit, lean, True), portions_of(amount, rows * top, limit, lean, False)
    places = jnp.arange(amount)

    def named(sizes, offset_by):
        used = int((sizes > 0).sum())
        fixed = max(1, used // 4)
        moved = fixed + (places - fixed + offset_by * (used - fixed)) % max(1, amount - fixed)
        return jnp.zeros((amount,), jnp.int32).at[sequence[jnp.where(places < fixed, places, moved)]].set(jnp.asarray(sizes, jnp.int32))

    sizes = jnp.where(number % 4 == 0, named(crowded, number // 4), named(ordinary, number - number // 4 - 1))
    mixed = jax.random.permutation(jax.random.fold_in(own, 3), amount)
    source_of, receiver = mixed[0:amount // 2 * 2:2], mixed[1:amount // 2 * 2:2]
    slack = jnp.minimum(sizes[source_of] - 1, limit - sizes[receiver]) // 2
    slack = jnp.where((source_of == sequence[0]) | (receiver == sequence[0]) | (sizes[receiver] == 0), 0, jnp.maximum(slack, 0))
    moved = jax.random.randint(jax.random.fold_in(own, 4), (amount // 2,), 0, 1 << 20) % (slack + 1)
    sizes = sizes.at[source_of].add(-moved).at[receiver].add(moved)
    members = jnp.searchsorted(jnp.cumsum(sizes), jnp.arange(rows * top), side="right").astype(jnp.int32)
    listing = members.reshape(top, rows).T
    listing = listing[jax.random.permutation(jax.random.fold_in(own, 1), rows)]
    offset_by = jax.random.randint(jax.random.fold_in(own, 2), (rows, 1), 0, top)
    return jnp.take_along_axis(listing, (jnp.arange(top)[None, :] + offset_by) % top, axis=1)


def portions_of(amount, total, limit, slope, full):
    portions = [(1 << 20) // math.isqrt(standing ** slope) + 1 for standing in range(1, amount + 1)]
    largest = limit if full else min(limit, max(-(-total // amount), total * portions[0] // sum(portions)))
    least = 1 if total - largest >= amount - 1 else 0
    given, spare = [largest] + [least] * (amount - 1), total - largest - least * (amount - 1)
    while spare > 0:
        free = [i for i in range(1, amount) if given[i] < largest] or [i for i in range(1, amount) if given[i] < limit]
        pool, budget = sum([portions[i] for i in free]), spare
        for i in free:
            extra = min(limit - given[i], max(1, budget * portions[i] // pool), spare)
            given[i] = given[i] + extra
            spare = spare - extra
    return np.array(given)


def normal_values(own_key, dims, width, most, shards=(), held_as=jnp.bfloat16):
    drawn = width * jax.random.normal(own_key, dims, jnp.float32)
    if shards:
        drawn = drawn * block_levels(own_key, dims, shards, -0.22, 0.18)
    return jnp.clip(drawn, -most, most).astype(held_as)


def setup_inputs(seed: int = 0) -> dict:
    key_of = jax.random.split(jax.random.key(seed), 8)
    in_flight = normal_values(key_of[0], (2, N_SECTION, TOKENS, D), 1.0, 6.0, ((1, 8), (2, 32)))
    entering = normal_values(key_of[1], (TICKS - 1, TOKENS, D), 1.0, 6.0, ((1, 32),))
    checkpoints = normal_values(key_of[2], (TICKS, 2, N_SECTION, TOKENS, D), 1.0, 6.0, ((2, 8), (3, 32)))
    expert_ids_keys = jax.random.split(jax.random.fold_in(key_of[3], 1), TICKS * 2 * N_SECTION * TOKENS // TOK_DEV)
    expert_ids_turns = jax.random.permutation(jax.random.fold_in(key_of[3], 3), TICKS * 2 * N_SECTION * TOKENS // TOK_DEV)
    expert_ids = jax.vmap(lambda own, number: shared_out(jax.random.fold_in(key_of[3], 2), own, number, TOK_DEV, EXPERTS, TOP, CAP, 1))(expert_ids_keys, expert_ids_turns).reshape((TICKS, 2, N_SECTION, TOKENS, TOP))
    gates = jnp.clip(0.1 + 0.9 * jax.random.uniform(key_of[4], (TICKS, 2, N_SECTION, TOKENS, TOP), jnp.float32) ** block_levels(key_of[4], (TICKS, 2, N_SECTION, TOKENS, TOP), ((2, 8), (3, 32)), -0.2, 0.2), 0.1, 1.0)
    w_in = normal_values(key_of[5], (2, N_SECTION, EXPERTS, D, FF), D ** -0.5, 0.15625, ((1, 8), (2, 8), (4, 4)))
    w_out = normal_values(key_of[6], (2, N_SECTION, EXPERTS, FF, D), FF ** -0.5, 0.15625, ((1, 8), (2, 8), (3, 4)))
    return dict(in_flight=in_flight, entering=entering, checkpoints=checkpoints, expert_ids=expert_ids, gates=gates, w_in=w_in, w_out=w_out)


def silu_parts(preact):
    squash = jax.nn.sigmoid(preact)
    return preact * squash, squash * (1.0 + preact * (1.0 - squash))


def slot_numbers(flat_ids, experts):
    onehot = (flat_ids[..., None] == jnp.arange(experts, dtype=jnp.int32)).astype(jnp.int32)
    before = jnp.cumsum(onehot, axis=-2) - onehot
    return jnp.sum(before * onehot, axis=-1).astype(jnp.int32)


def expert_rows(rows_x, rows_g, weight_in, weight_out):
    preact = jnp.dot(rows_x, weight_in, preferred_element_type=jnp.float32)
    hidden_grad = lax.dot_general(rows_g, weight_out, (((1,), (1,)), ((), ())), preferred_element_type=jnp.float32)
    activated, slope_grad = silu_parts(preact)
    preact_grad = (hidden_grad * slope_grad).astype(jnp.bfloat16)
    activated = activated.astype(jnp.bfloat16)
    shard_width = weight_in.shape[1] // N_DP
    partial_sum = jnp.zeros((rows_x.shape[0], weight_in.shape[0]), jnp.float32)
    for shard_index in range(N_DP):
        lower_edge = shard_index * shard_width
        shard_term = lax.dot_general(preact_grad[:, lower_edge:lower_edge + shard_width], weight_in[:, lower_edge:lower_edge + shard_width], (((1,), (1,)), ((), ())), preferred_element_type=jnp.float32)
        shard_term = lax.optimization_barrier(shard_term.astype(jnp.bfloat16))
        partial_sum = partial_sum + shard_term.astype(jnp.float32)
    routed_grad = partial_sum.astype(jnp.bfloat16)
    grad_in = lax.dot_general(rows_x, preact_grad, (((0,), (0,)), ((), ())), preferred_element_type=jnp.float32)
    grad_out = lax.dot_general(activated, rows_g, (((0,), (0,)), ((), ())), preferred_element_type=jnp.float32)
    return routed_grad, grad_in, grad_out


def position_step(incoming, inputs, route_ids, route_gates, weight_in, weight_out):
    tokens_all = incoming.shape[0]
    fanout = route_ids.shape[1]
    features = incoming.shape[1]
    blocks = tokens_all // TOK_DEV
    experts = weight_in.shape[0]
    slot_index = slot_numbers(route_ids.reshape(blocks, TOK_DEV * fanout), experts).reshape(tokens_all, fanout)
    source = (jnp.arange(tokens_all, dtype=jnp.int32) // TOK_DEV)[:, None]
    row_index = (source * CAP + slot_index).astype(jnp.int32)
    scaled = (route_gates[:, :, None] * incoming[:, None, :].astype(jnp.float32)).astype(jnp.bfloat16)
    copies = jnp.broadcast_to(inputs[:, None, :], scaled.shape)
    buffer_x = jnp.zeros((experts, blocks * CAP, features), inputs.dtype).at[route_ids, row_index].set(copies)
    buffer_g = jnp.zeros((experts, blocks * CAP, features), scaled.dtype).at[route_ids, row_index].set(scaled)
    routed_grad, grad_in, grad_out = lax.map(lambda packed: expert_rows(*packed), (buffer_x, buffer_g, weight_in, weight_out))
    contrib = routed_grad[route_ids, row_index].astype(jnp.float32)
    result = (incoming.astype(jnp.float32) + jnp.sum(contrib, axis=1)).astype(jnp.bfloat16)
    return result, grad_in, grad_out


def reference(in_flight, entering, checkpoints, expert_ids, gates, w_in, w_out):
    sections = N_SECTION
    positions = 2 * sections
    flat_w_in = w_in.reshape((positions,) + w_in.shape[2:])
    flat_w_out = w_out.reshape((positions,) + w_out.shape[2:])

    def results_only(packed):
        return position_step(*packed)[0]

    def flatten(stacked):
        return stacked.reshape((positions,) + stacked.shape[2:])

    incoming = in_flight
    received = []
    produced = []
    for tick_index in range(TICKS):
        received.append(incoming)
        result = lax.map(results_only, (flatten(incoming), flatten(checkpoints[tick_index]), flatten(expert_ids[tick_index]), flatten(gates[tick_index]), flat_w_in, flat_w_out))
        result = result.reshape(incoming.shape)
        produced.append(result)
        if tick_index + 1 < TICKS:
            upper_grad = jnp.concatenate([entering[tick_index][None], result[1, :-1]], axis=0)
            lower_grad = jnp.concatenate([result[0, 1:], result[1, -1:]], axis=0)
            incoming = jnp.stack([lower_grad, upper_grad])
    out_grads = jnp.stack(produced)
    history = jnp.stack(received)

    def by_position(stacked):
        return jnp.moveaxis(stacked.reshape((TICKS, positions) + stacked.shape[3:]), 0, 1)

    def weight_grads(packed):
        inputs_all, saved_all, ids_all, gates_all, weight_in, weight_out = packed
        total_in = jnp.zeros(weight_in.shape, jnp.float32)
        total_out = jnp.zeros(weight_out.shape, jnp.float32)
        for tick_index in range(TICKS):
            unused, grad_in, grad_out = position_step(inputs_all[tick_index], saved_all[tick_index], ids_all[tick_index], gates_all[tick_index], weight_in, weight_out)
            total_in = total_in + grad_in
            total_out = total_out + grad_out
        return total_in.astype(jnp.bfloat16), total_out.astype(jnp.bfloat16)

    grad_in, grad_out = lax.map(weight_grads, (by_position(history), by_position(checkpoints), by_position(expert_ids), by_position(gates), flat_w_in, flat_w_out))
    return out_grads, grad_in.reshape(w_in.shape), grad_out.reshape(w_out.shape)
```

```python
import jax
import jax.numpy as jnp
from jax import lax
from jax.experimental import pallas as pl
from jax.experimental.pallas import tpu as pltpu
from jax.sharding import PartitionSpec as P

MESH = pl.DeviceIdType.MESH
BF, F32, I32 = jnp.bfloat16, jnp.float32, jnp.int32


def iota(shape, dim):
    return lax.broadcasted_iota(I32, shape, dim)


def ones_at(cond):
    return jnp.where(cond, 1.0, 0.0).astype(BF)


def dot(a, b, dims=((1,), (0,))):
    return lax.dot_general(a, b, (dims, ((), ())), preferred_element_type=F32)


def kernel(
    flight, entering, chk, ids, gat, idc, w_in, w_out,
    out, gin, gout,
    W1, W2, XT, XS, XST, XB, XTR, IDX, GS, GR, GB, PG, AC, PR, RA, SB, FR, RS, RR, INC, RES, SELG, SELP, WG1, WG2,
    send_sem, loc_sem, id_sem, xa_sem, xf_sem, xm_sem, xt_sem, gx_sem, ga_sem, gf_sem, r1_sem, re_sem, r2_sem, rr_sem, z_sem,
    w_sem, o_sem,
):
    D = flight.shape[2]
    H = D // 2
    NJ = D // 128
    Q = D // 4
    z, e, y = (lax.axis_index(a) for a in ("section", "expert", "dp"))
    yn, yp, y2 = lax.rem(y + 1, 4), lax.rem(y + 3, 4), lax.rem(y + 2, 4)
    above, below, across = (z, e, yn), (z, e, yp), (z, e, y2)
    z_up, z_down = (lax.rem(z + 1, 8), e, y), (lax.rem(z + 7, 8), e, y)
    peers = [lax.rem(e + k, 8) for k in (1, 7, 2, 6, 3, 5, 4)]

    sends, locals_ = [], []

    def send(src, dst, sem, device):
        copy = pltpu.make_async_remote_copy(
            src_ref=src, dst_ref=dst, send_sem=send_sem.at[len(sends)], recv_sem=sem,
            device_id=device, device_id_type=MESH,
        )
        copy.start()
        sends.append(copy)

    def arrived(ref, sem):
        pltpu.make_async_copy(ref, ref, sem).wait()

    weights = []
    for c in (1, 0):
        weights.append((
            pltpu.make_async_copy(w_in.at[c], W1.at[c], w_sem.at[c, 0]),
            pltpu.make_async_copy(w_out.at[c], W2.at[c], w_sem.at[c, 1]),
        ))
        for copy in weights[-1]:
            copy.start()

    barrier = pltpu.get_barrier_semaphore()
    greeted = [(z, p, y) for p in peers] + [above, below, across, z_up, z_down]
    for device in greeted:
        pl.semaphore_signal(barrier, inc=1, device_id=device, device_id_type=MESH)

    for i in range(4):
        XT[i, y] = chk[i]
    IDX[y] = ids[:, 0:128]
    row, col = iota((384, 512), 0), iota((384, 512), 1)
    SELG[...] = ones_at(((row >> 5) == (col & 15)) & (((row >> 2) & 7) == ((col >> 4) & 7)) & ((row & 3) == (col >> 7)))
    row, col = iota((512, 384), 0), iota((512, 384), 1)
    SELP[...] = ones_at(((col >> 5) == (row & 15)) & (((col >> 2) & 7) == ((row >> 4) & 7)) & ((col & 3) == (row >> 7)))

    pl.semaphore_wait(barrier, len(greeted))

    def ids_send():
        for n, device in enumerate((above, below, across)):
            send(IDX.at[y], IDX.at[y], id_sem.at[n], device)

    def ids_wait():
        for n, b in enumerate((yp, yn, y2)):
            arrived(IDX.at[b], id_sem.at[n])

    def x_send(i):
        send(XT.at[i, y], XT.at[i, y], xa_sem.at[i, 0], above)
        send(XT.at[i, y], XT.at[i, y], xa_sem.at[i, 1], below)

    def x_forward(i):
        arrived(XT.at[i, yp], xa_sem.at[i, 0])
        half = XT.at[i, yp, pl.ds(0, 16)]
        send(half, half, xf_sem.at[i, 0], above)
        arrived(XT.at[i, yn], xa_sem.at[i, 1])
        half = XT.at[i, yn, pl.ds(16, 16)]
        send(half, half, xf_sem.at[i, 1], below)

    def x_dispatch(i):
        c, t = i // 2, i % 2
        r = 2 * (2 * t + c)
        arrived(XT.at[i, y2, pl.ds(0, 16)], xf_sem.at[i, 0])
        arrived(XT.at[i, y2, pl.ds(16, 16)], xf_sem.at[i, 1])
        lane = iota((8, 128), 1) >> 5
        every = jnp.where(lane == 0, IDX[0], jnp.where(lane == 1, IDX[1], jnp.where(lane == 2, IDX[2], IDX[3])))
        id0, id1 = every[r:r + 1], every[r + 1:r + 2]
        a, b = iota((128, 128), 0), iota((128, 128), 1)
        upper = ones_at(((a >> 5) == (b >> 5)) & (a < b))
        tokens = XT[i].reshape(128, D)
        row, col = iota((256, 128), 0), iota((256, 128), 1)
        member = ((id0 == (row >> 5)) | (id1 == (row >> 5))) & (((row >> 3) & 3) == (col >> 5))
        before = dot(ones_at(member), upper)
        hit = member & (before == (row & 7).astype(F32))
        XS[i] = dot(ones_at(hit), tokens).astype(BF).reshape(8, 32, D)
        row, col = iota((128, 128), 0), iota((128, 128), 1)
        member = ((id0 == (row >> 4)) | (id1 == (row >> 4))) & ((row & 3) == (col >> 5))
        before = dot(ones_at(member), upper)
        hit = member & (before == 8.0)
        wide = jnp.concatenate([ones_at(hit & (((row >> 2) & 3) == q)) for q in range(4)], axis=1)
        stacked = jnp.concatenate([tokens[:, Q * q:Q * q + Q] for q in range(4)], axis=0)
        XST[i] = dot(wide, stacked).astype(BF).reshape(8, 16, Q)
        for p in peers:
            send(XS.at[i, p], XB.at[i, e], xm_sem.at[i], (z, p, y))
            send(XST.at[i, p], XTR.at[i, e], xt_sem.at[i], (z, p, y))
        pltpu.make_async_copy(XS.at[i, e], XB.at[i, e], xm_sem.at[i]).start()
        pltpu.make_async_copy(XST.at[i, e], XTR.at[i, e], xt_sem.at[i]).start()

    def x_finish(i):
        arrived(XB.at[i, pl.ds(0, 8)], xm_sem.at[i])
        arrived(XTR.at[i], xt_sem.at[i])
        row, col = iota((128, 128), 0), iota((128, 128), 1)
        pick = ones_at(((row >> 5) == ((col >> 2) & 3)) & (((row >> 2) & 7) == (col >> 4)) & ((row & 3) == (col & 3)))
        rows = dot(pick, XTR[i].reshape(128, Q)).astype(BF)
        for q in range(4):
            XB[i, 8, :, Q * q:Q * q + Q] = rows[32 * q:32 * q + 32]

    def g_dispatch(i, incoming):
        c, t = i // 2, i % 2
        r = 2 * (2 * t + c)
        id0, id1 = ids[r:r + 1, 0:32], ids[r + 1:r + 2, 0:32]
        g0, g1 = gat[r:r + 1, :], gat[r + 1:r + 2, :]
        upper = ones_at(iota((32, 32), 0) < iota((32, 32), 1))
        row = iota((64, 32), 0)
        first = id0 == (row >> 3)
        member = first | (id1 == (row >> 3))
        before = dot(ones_at(member), upper)
        hit = member & (before == (row & 7).astype(F32))
        gate = jnp.sum(jnp.where(hit, jnp.where(first, g0, g1), 0.0), axis=1, keepdims=True)
        main = (dot(ones_at(hit), incoming) * gate).reshape(8, 8, D)
        GS[i, :, :, 0:H] = jnp.concatenate([main[:, :, :H], main[:, :, H:]], axis=1).astype(BF)
        row = iota((128, 32), 0)
        first = id0 == (row >> 4)
        member = first | (id1 == (row >> 4))
        counted = ones_at(member)
        before = dot(counted, upper)
        gate = jnp.sum(jnp.where(member & (before == 8.0), jnp.where(first, g0, g1), 0.0), axis=1, keepdims=True)
        row, col = iota((128, 32 * NJ), 0), iota((128, 32 * NJ), 1)
        wide0, wide1 = ids[r:r + 1, :], ids[r + 1:r + 2, :]
        member = (wide0 == (row >> 4)) | (wide1 == (row >> 4))
        upper = ones_at(iota((32, 32 * NJ), 0) < (iota((32, 32 * NJ), 1) & 31))
        before = dot(counted, upper)
        hit = member & (before == 8.0) & ((row & 15) == (col >> 5))
        stacked = jnp.concatenate([incoming[:, 128 * j:128 * j + 128] for j in range(NJ)], axis=0)
        GS[i, :, :, H:H + 128] = (dot(ones_at(hit), stacked) * gate).astype(BF).reshape(8, 16, 128)
        part = e >> 2
        for p in peers:
            send(GS.at[i, p], GR.at[i, y, e], gx_sem.at[i, part], (z, p, y))
        pltpu.make_async_copy(GS.at[i, e], GR.at[i, y, e], gx_sem.at[i, part]).start()

    def g_first(i):
        lower, upper = GR.at[i, y, pl.ds(0, 4)], GR.at[i, y, pl.ds(4, 4)]
        arrived(lower, gx_sem.at[i, 0])
        send(lower, lower, ga_sem.at[i, 0, 0], above)
        arrived(upper, gx_sem.at[i, 1])
        send(upper, upper, ga_sem.at[i, 1, 1], below)
        send(upper, upper, ga_sem.at[i, 0, 1], above)
        send(lower, lower, ga_sem.at[i, 1, 0], below)

    def g_second(i):
        lower, upper = GR.at[i, yp, pl.ds(0, 4)], GR.at[i, yn, pl.ds(4, 4)]
        arrived(lower, ga_sem.at[i, 0, 0])
        send(lower, lower, gf_sem.at[i, 0], above)
        arrived(upper, ga_sem.at[i, 1, 1])
        send(upper, upper, gf_sem.at[i, 1], below)

    def g_finish(i):
        arrived(GR.at[i, yp, pl.ds(4, 4)], ga_sem.at[i, 0, 1])
        arrived(GR.at[i, yn, pl.ds(0, 4)], ga_sem.at[i, 1, 0])
        arrived(GR.at[i, y2, pl.ds(0, 4)], gf_sem.at[i, 0])
        arrived(GR.at[i, y2, pl.ds(4, 4)], gf_sem.at[i, 1])

        @pl.loop(0, 8)
        def _(s):
            folded = GR[i, :, s, :, 0:H].astype(F32)
            GB[i, s, :, 0:H] = folded[:, 0:8].reshape(32, H).astype(BF)
            GB[i, s, :, H:D] = folded[:, 8:16].reshape(32, H).astype(BF)

        tails = dot(SELG[...], GR[i, :, :, :, H:H + 128].reshape(512, 128)).astype(BF)
        for j in range(NJ):
            GB[i, 8, :, 128 * j:128 * j + 128] = tails[32 * j:32 * j + 32]

    def compute(i):
        c = i // 2
        preact = dot(XB[i].reshape(288, D), W1[c])
        hidden = dot(GB[i].reshape(288, D), W2[c], ((1,), (1,)))
        squash = 1.0 / (1.0 + jnp.exp(-preact))
        AC[i] = (preact * squash).astype(BF)
        grad = (hidden * (squash * (1.0 + preact * (1.0 - squash)))).astype(BF)
        PG[i] = grad
        main = grad[0:256]
        left = dot(main, W1[c, 0:H], ((1,), (1,))).reshape(8, 4, 8, H)
        right = dot(main, W1[c, H:D], ((1,), (1,))).reshape(8, 4, 8, H)
        for b in range(4):
            PR[i, b, :, :, 0:H] = jnp.concatenate([left[:, b], right[:, b]], axis=1).astype(BF)
        tail = dot(grad[256:288], W1[c], ((1,), (1,))).astype(BF)
        stacked = jnp.concatenate([tail[:, 128 * j:128 * j + 128] for j in range(NJ)], axis=0)
        PR[i, :, :, :, H:H + 128] = dot(SELP[...], stacked).astype(BF).reshape(4, 8, 16, 128)

    def r_first(i):
        send(PR.at[i, y2, pl.ds(0, 4)], RA.at[i, 0], r1_sem.at[i, 0], above)
        send(PR.at[i, y2, pl.ds(4, 4)], RA.at[i, 1], r1_sem.at[i, 1], below)
        send(PR.at[i, yn, pl.ds(4, 4)], FR.at[i, 0, pl.ds(4, 4)], re_sem.at[i, 0], above)
        send(PR.at[i, yp, pl.ds(0, 4)], FR.at[i, 1, pl.ds(0, 4)], re_sem.at[i, 1], below)

    def r_second(i):
        arrived(RA.at[i, 0], r1_sem.at[i, 0])
        SB[i, 0] = (PR[i, yn, 0:4].astype(F32) + RA[i, 0].astype(F32)).astype(BF)
        send(SB.at[i, 0], FR.at[i, 0, pl.ds(0, 4)], r2_sem.at[i, 0], above)
        arrived(RA.at[i, 1], r1_sem.at[i, 1])
        SB[i, 1] = (PR[i, yp, 4:8].astype(F32) + RA[i, 1].astype(F32)).astype(BF)
        send(SB.at[i, 1], FR.at[i, 1, pl.ds(4, 4)], r2_sem.at[i, 1], below)

    def r_third(i):
        arrived(FR.at[i, 0, pl.ds(4, 4)], re_sem.at[i, 0])
        arrived(FR.at[i, 1, pl.ds(0, 4)], re_sem.at[i, 1])
        arrived(FR.at[i, 0, pl.ds(0, 4)], r2_sem.at[i, 0])
        arrived(FR.at[i, 1, pl.ds(4, 4)], r2_sem.at[i, 1])
        RS[i] = (PR[i, y].astype(F32) + FR[i, 0].astype(F32) + FR[i, 1].astype(F32)).astype(BF)
        for p in peers:
            send(RS.at[i, p], RR.at[i, e], rr_sem.at[i], (z, p, y))
        pltpu.make_async_copy(RS.at[i, e], RR.at[i, e], rr_sem.at[i]).start()

    def r_fourth(i, incoming):
        c, t = i // 2, i % 2
        id0, id1 = idc[2 * t + c, :, 0:1], idc[2 * t + c, :, 1:2]
        col = iota((32, 128), 1)
        member = (id0 == (col >> 4)) | (id1 == (col >> 4))
        before = dot(ones_at(iota((32, 32), 1) < iota((32, 32), 0)), ones_at(member))
        hit = member & (before == (col & 7).astype(F32))
        side = (col >> 3) & 1
        pick = jnp.concatenate([ones_at(hit & (side == 0)), ones_at(hit & (side == 1))], axis=0)
        last = member & (before == 8.0)
        pick_last = jnp.concatenate([ones_at(last & ((col & 15) == j)) for j in range(NJ)], axis=0)
        arrived(RR.at[i], rr_sem.at[i])
        main = dot(pick, RR[i, :, :, 0:H].reshape(128, H))
        tail = dot(pick_last, RR[i, :, :, H:H + 128].reshape(128, 128))
        for j in range(NJ):
            side = 128 * j // H
            at = 128 * j - side * H
            RES[i, :, 128 * j:128 * j + 128] = (
                incoming[:, 128 * j:128 * j + 128].astype(F32)
                + (main[32 * side:32 * side + 32, at:at + 128] + tail[32 * j:32 * j + 32])
            ).astype(BF)
        out[2 * t + c] = RES[i]

    outs = []

    def weight_grads(c):
        grad = PG[2 * c:2 * c + 2].reshape(576, -1)

        @pl.loop(0, D // 256)
        def _(n):
            at = pl.ds(pl.multiple_of(n * 256, 256), 256)
            WG1[c, at, :] = dot(XB[2 * c:2 * c + 2, :, :, at].reshape(576, 256), grad, ((0,), (0,))).astype(BF)

        copy = pltpu.make_async_copy(WG1.at[c], gin.at[c], o_sem.at[c, 0])
        copy.start()
        outs.append(copy)
        act = AC[2 * c:2 * c + 2].reshape(576, -1)

        @pl.loop(0, D // 512)
        def _(n):
            at = pl.ds(pl.multiple_of(n * 512, 512), 512)
            WG2[c, :, at] = dot(act, GB[2 * c:2 * c + 2, :, :, at].reshape(576, 512), ((0,), (0,))).astype(BF)

        copy = pltpu.make_async_copy(WG2.at[c], gout.at[c], o_sem.at[c, 1])
        copy.start()
        outs.append(copy)

    A, B, C, E = 2, 0, 3, 1
    ids_send()
    x_send(A)
    x_send(B)
    g_dispatch(A, flight[1])
    g_dispatch(B, flight[0])
    ids_wait()
    x_forward(A)
    x_forward(B)
    g_first(A)
    x_dispatch(A)
    g_second(A)
    g_first(B)
    x_dispatch(B)
    for copy in weights[0] + weights[1]:
        copy.wait()
    x_finish(A)
    g_finish(A)
    compute(A)
    r_first(A)
    g_second(B)
    x_send(C)
    x_finish(B)
    g_finish(B)
    r_second(A)
    compute(B)
    r_first(B)
    x_send(E)
    x_forward(C)
    r_third(A)
    r_second(B)
    r_fourth(A, flight[1])
    send(RES.at[A], INC.at[1], z_sem.at[1], z_up)
    x_dispatch(C)
    r_third(B)
    x_forward(E)
    arrived(INC.at[1], z_sem.at[1])
    upper = jnp.where(z == 0, entering[...], INC[1])
    g_dispatch(C, upper)
    r_fourth(B, flight[0])
    send(RES.at[B], INC.at[0], z_sem.at[0], z_down)
    g_first(C)
    arrived(INC.at[0], z_sem.at[0])
    lower = jnp.where(z == 7, RES[A], INC[0])
    g_dispatch(E, lower)
    x_dispatch(E)
    g_second(C)
    g_first(E)
    x_finish(C)
    g_finish(C)
    compute(C)
    r_first(C)
    g_second(E)
    x_finish(E)
    g_finish(E)
    r_second(C)
    compute(E)
    r_first(E)
    weight_grads(1)
    r_third(C)
    r_second(E)
    r_fourth(C, upper)
    weight_grads(0)
    r_third(E)
    r_fourth(E, lower)
    for copy in sends:
        copy.wait_send()
    for copy in outs:
        copy.wait()


def per_device(in_flight, entering, checkpoints, expert_ids, gates, w_in, w_out):
    D = in_flight.shape[-1]
    F = w_in.shape[-1]
    T = 4
    W = D // 2 + 128
    by_layer = checkpoints[:, :, 0].swapaxes(0, 1).reshape(T, 32, D)
    ids = expert_ids[:, :, 0]
    ids_rows = jnp.tile(ids.swapaxes(2, 3).reshape(2 * T, 32), (1, D // 128))
    gate_rows = gates[:, :, 0].swapaxes(2, 3).reshape(2 * T, 32)
    ids_columns = ids.reshape(T, 32, 2)
    vmem, anywhere = pl.BlockSpec(memory_space=pltpu.VMEM), pl.BlockSpec(memory_space=pl.ANY)
    dma = pltpu.SemaphoreType.DMA
    out, gin, gout = pl.pallas_call(
        kernel,
        out_shape=(
            jax.ShapeDtypeStruct((T, 32, D), BF),
            jax.ShapeDtypeStruct((2, D, F), BF),
            jax.ShapeDtypeStruct((2, F, D), BF),
        ),
        in_specs=[vmem] * 6 + [anywhere] * 2,
        out_specs=(vmem, anywhere, anywhere),
        scratch_shapes=[
            pltpu.VMEM((2, D, F), BF),
            pltpu.VMEM((2, F, D), BF),
            pltpu.VMEM((T, 4, 32, D), BF),
            pltpu.VMEM((T, 8, 32, D), BF),
            pltpu.VMEM((T, 8, 16, D // 4), BF),
            pltpu.VMEM((T, 9, 32, D), BF),
            pltpu.VMEM((T, 8, 16, D // 4), BF),
            pltpu.VMEM((4, 8, 128), I32),
            pltpu.VMEM((T, 8, 16, W), BF),
            pltpu.VMEM((T, 4, 8, 16, W), BF),
            pltpu.VMEM((T, 9, 32, D), BF),
            pltpu.VMEM((T, 288, F), BF),
            pltpu.VMEM((T, 288, F), BF),
            pltpu.VMEM((T, 4, 8, 16, W), BF),
            pltpu.VMEM((T, 2, 4, 16, W), BF),
            pltpu.VMEM((T, 2, 4, 16, W), BF),
            pltpu.VMEM((T, 2, 8, 16, W), BF),
            pltpu.VMEM((T, 8, 16, W), BF),
            pltpu.VMEM((T, 8, 16, W), BF),
            pltpu.VMEM((2, 32, D), BF),
            pltpu.VMEM((T, 32, D), BF),
            pltpu.VMEM((384, 512), BF),
            pltpu.VMEM((512, 384), BF),
            pltpu.VMEM((2, D, F), BF),
            pltpu.VMEM((2, F, D), BF),
            dma((200,)), dma((1,)), dma((3,)),
            dma((T, 2)), dma((T, 2)), dma((T,)), dma((T,)),
            dma((T, 2)), dma((T, 2, 2)), dma((T, 2)),
            dma((T, 2)), dma((T, 2)), dma((T, 2)), dma((T,)), dma((2,)),
            dma((2, 2)), dma((2, 2)),
        ],
        compiler_params=pltpu.CompilerParams(
            collective_id=0, has_side_effects=True, vmem_limit_bytes=60 * 2**20
        ),
    )(in_flight[:, 0], entering[0], by_layer, ids_rows, gate_rows, ids_columns, w_in[:, 0, 0], w_out[:, 0, 0])
    return out.reshape(2, 2, 1, 32, D), gin[:, None, None], gout[:, None, None]


def solution(mesh):
    tokens = P(None, None, "section", ("expert", "dp"), None)
    weight_in = P(None, "section", "expert", None, "dp")
    weight_out = P(None, "section", "expert", "dp", None)
    return jax.shard_map(
        per_device,
        mesh=mesh,
        in_specs=(P(None, "section", ("expert", "dp"), None), P(None, ("expert", "dp"), None), tokens, tokens, tokens,
                  weight_in, weight_out),
        out_specs=(tokens, weight_in, weight_out),
        check_vma=False,
    )
```

```python
import jax
import jax.numpy as jnp
from jax import lax
from jax.experimental import pallas as pl
from jax.experimental.pallas import tpu as pltpu
from jax.sharding import PartitionSpec as P

MESH = pl.DeviceIdType.MESH
BF, F32, I32 = jnp.bfloat16, jnp.float32, jnp.int32
NC = 2


def iota(shape, dim):
    return lax.broadcasted_iota(I32, shape, dim)


def ones_at(cond):
    return jnp.where(cond, 1.0, 0.0).astype(BF)


def dot(a, b, dims=((1,), (0,))):
    return lax.dot_general(a, b, (dims, ((), ())), preferred_element_type=F32)


def kernel(
    flight_in, entering_in, chk, ids_own, gat, w_in, w_out,
    out, gin, gout,
    flight, entering,
    W1, W2, XT, XS, XST, XB, XTR, IDX, GS, GR, GB, PG, AC, PR, RA, SB, FR, RS, RR, INC, RES, SELG, SELP, WG1, WG2, ids, idc, DG, GT, DL, GL, PK, PL, OUT,
    send_sem, loc_sem, id_sem, xa_sem, xf_sem, xm_sem, xt_sem, gx_sem, ga_sem, gf_sem, r1_sem, re_sem, r2_sem, rr_sem, z_sem,
    w_sem, o_sem, out_sem,
):
    D = flight.shape[2]
    H = D // 2
    K = H // NC
    to_expert = [pl.ds(K * k, K + 128 * (k == NC - 1)) for k in range(NC)]
    back = [pl.ds(128 * (k > 0) + K * k, K + 128 * (k == 0)) for k in range(NC)]
    NJ = D // 128
    Q = D // 4
    z, e, y = (lax.axis_index(a) for a in ("section", "expert", "dp"))
    yn, yp, y2 = lax.rem(y + 1, 4), lax.rem(y + 3, 4), lax.rem(y + 2, 4)
    above, below, across = (z, e, yn), (z, e, yp), (z, e, y2)
    z_up, z_down = (lax.rem(z + 1, 8), e, y), (lax.rem(z + 7, 8), e, y)
    peers = [lax.rem(e + k, 8) for k in (1, 7, 2, 6, 3, 5, 4)]

    sends, outs = [], []

    def send(src, dst, sem, device):
        copy = pltpu.make_async_remote_copy(
            src_ref=src, dst_ref=dst, send_sem=send_sem.at[len(sends)], recv_sem=sem,
            device_id=device, device_id_type=MESH,
        )
        copy.start()
        sends.append(copy)

    def arrived(ref, sem):
        pltpu.make_async_copy(ref, ref, sem).wait()

    barrier = pltpu.get_barrier_semaphore()
    greeted = [(z, p, y) for p in peers] + [above, below, across, z_up, z_down]
    for device in greeted:
        pl.semaphore_signal(barrier, inc=1, device_id=device, device_id_type=MESH)

    loads = [pltpu.make_async_copy(chk.at[2 * (i % 2) + i // 2], XT.at[i, y], loc_sem.at[i]) for i in range(4)]
    loads.append(pltpu.make_async_copy(flight_in, flight, loc_sem.at[4]))
    loads.append(pltpu.make_async_copy(entering_in, entering, loc_sem.at[5]))
    for copy in loads:
        copy.start()

    weights = []
    for c in (1, 0):
        weights.append((
            pltpu.make_async_copy(w_in.at[c], W1.at[c], w_sem.at[c, 0]),
            pltpu.make_async_copy(w_out.at[c], W2.at[c], w_sem.at[c, 1]),
        ))
        for copy in weights[-1]:
            copy.start()

    narrow = ids_own[...].astype(F32).astype(BF)
    ids[...] = dot(narrow, ones_at(iota((32, 32 * NJ), 0) == (iota((32, 32 * NJ), 1) & 31))).astype(I32)
    idc[...] = dot(ones_at(iota((32, 32), 0) == iota((32, 32), 1)), narrow, ((1,), (1,))).astype(I32)
    IDX[y] = ids[:, 0:128]
    row, col = iota((384, 512), 0), iota((384, 512), 1)
    SELG[...] = ones_at(((row >> 5) == (col & 15)) & (((row >> 2) & 7) == ((col >> 4) & 7)) & ((row & 3) == (col >> 7)))
    row, col = iota((512, 384), 0), iota((512, 384), 1)
    SELP[...] = ones_at(((col >> 5) == (row & 15)) & (((col >> 2) & 7) == ((row >> 4) & 7)) & ((col & 3) == (row >> 7)))

    def ids_send():
        for n, device in enumerate((above, below, across)):
            send(IDX.at[y], IDX.at[y], id_sem.at[n], device)

    def ids_wait():
        for n, b in enumerate((yp, yn, y2)):
            arrived(IDX.at[b], id_sem.at[n])

    def x_send(i):
        send(XT.at[i, y], XT.at[i, y], xa_sem.at[i, 0], above)
        send(XT.at[i, y], XT.at[i, y], xa_sem.at[i, 1], below)

    def x_forward(i):
        arrived(XT.at[i, yp], xa_sem.at[i, 0])
        half = XT.at[i, yp, pl.ds(0, 16)]
        send(half, half, xf_sem.at[i, 0], above)
        arrived(XT.at[i, yn], xa_sem.at[i, 1])
        half = XT.at[i, yn, pl.ds(16, 16)]
        send(half, half, xf_sem.at[i, 1], below)

    def x_dispatch(i, n):
        c, t = i // 2, i % 2
        r = 2 * (2 * t + c)
        a, b = iota((128, 128), 0), iota((128, 128), 1)
        upper = ones_at(((a >> 5) == (b >> 5)) & (a < b))
        pair = y // 2 if n == 0 else 1 - y // 2
        if n:
            arrived(XT.at[i, y2, pl.ds(0, 16)], xf_sem.at[i, 0])
            arrived(XT.at[i, y2, pl.ds(16, 16)], xf_sem.at[i, 1])
        both = jnp.where(iota((8, 128), 1) < 32, IDX[2 * pair], IDX[2 * pair + 1])
        id0, id1 = both[r:r + 1, 0:64], both[r + 1:r + 2, 0:64]
        row, col = iota((128, 64), 0), iota((128, 64), 1)
        member = ((id0 == (row >> 4)) | (id1 == (row >> 4))) & (((row >> 3) & 1) == (col >> 5))
        before = dot(ones_at(member), upper[0:64, 0:64])
        hit = member & (before == (row & 7).astype(F32))
        XS[i, pair] = dot(ones_at(hit), XT[i, pl.ds(2 * pair, 2)].reshape(64, D)).astype(BF).reshape(8, 16, D)
        rows = pl.ds(pl.multiple_of(16 * pair, 16), 16)
        for p in peers:
            send(XS.at[i, pair, p], XB.at[i, e, rows], xm_sem.at[i], (z, p, y))
        pltpu.make_async_copy(XS.at[i, pair, e], XB.at[i, e, rows], xm_sem.at[i]).start()
        if n:
            tokens = XT[i].reshape(128, D)
            lane = iota((8, 128), 1) >> 5
            every = jnp.where(lane == 0, IDX[0], jnp.where(lane == 1, IDX[1], jnp.where(lane == 2, IDX[2], IDX[3])))
            id0, id1 = every[r:r + 1], every[r + 1:r + 2]
            row, col = iota((128, 128), 0), iota((128, 128), 1)
            member = ((id0 == (row >> 4)) | (id1 == (row >> 4))) & ((row & 3) == (col >> 5))
            before = dot(ones_at(member), upper)
            hit = member & (before == 8.0)
            wide = jnp.concatenate([ones_at(hit & (((row >> 2) & 3) == q)) for q in range(4)], axis=1)
            stacked = jnp.concatenate([tokens[:, Q * q:Q * q + Q] for q in range(4)], axis=0)
            XST[i] = dot(wide, stacked).astype(BF).reshape(8, 16, Q)
            for p in peers:
                send(XST.at[i, p], XTR.at[i, e], xt_sem.at[i], (z, p, y))
            pltpu.make_async_copy(XST.at[i, e], XTR.at[i, e], xt_sem.at[i]).start()

    def x_finish(i):
        arrived(XB.at[i, pl.ds(0, 8)], xm_sem.at[i])
        arrived(XTR.at[i], xt_sem.at[i])
        row, col = iota((128, 128), 0), iota((128, 128), 1)
        pick = ones_at(((row >> 5) == ((col >> 2) & 3)) & (((row >> 2) & 7) == (col >> 4)) & ((row & 3) == (col & 3)))
        rows = dot(pick, XTR[i].reshape(128, Q)).astype(BF)
        for q in range(4):
            XB[i, 8, :, Q * q:Q * q + Q] = rows[32 * q:32 * q + 32]

    def prepare(i):
        c, t = i // 2, i % 2
        r = 2 * (2 * t + c)
        id0, id1 = ids[r:r + 1, 0:32], ids[r + 1:r + 2, 0:32]
        g0, g1 = gat[r:r + 1, :], gat[r + 1:r + 2, :]
        upper = ones_at(iota((32, 32), 0) < iota((32, 32), 1))
        row = iota((64, 32), 0)
        first = id0 == (row >> 3)
        member = first | (id1 == (row >> 3))
        before = dot(ones_at(member), upper)
        hit = member & (before == (row & 7).astype(F32))
        gate = jnp.sum(jnp.where(hit, jnp.where(first, g0, g1), 0.0), axis=1, keepdims=True)
        DG[i] = ones_at(hit)
        GT[i] = jnp.broadcast_to(gate, (64, 128))
        row = iota((128, 32), 0)
        first = id0 == (row >> 4)
        member = first | (id1 == (row >> 4))
        counted = ones_at(member)
        before = dot(counted, upper)
        gate = jnp.sum(jnp.where(member & (before == 8.0), jnp.where(first, g0, g1), 0.0), axis=1, keepdims=True)
        row, col = iota((128, 32 * NJ), 0), iota((128, 32 * NJ), 1)
        wide0, wide1 = ids[r:r + 1, :], ids[r + 1:r + 2, :]
        member = (wide0 == (row >> 4)) | (wide1 == (row >> 4))
        upper = ones_at(iota((32, 32 * NJ), 0) < (iota((32, 32 * NJ), 1) & 31))
        before = dot(counted, upper)
        DL[i] = ones_at(member & (before == 8.0) & ((row & 15) == (col >> 5)))
        GL[i] = jnp.broadcast_to(gate, (128, 128))

    def prepare_return(i):
        c, t = i // 2, i % 2
        r = 2 * (2 * t + c)
        id0, id1 = idc[:, r:r + 1], idc[:, r + 1:r + 2]
        col = iota((32, 128), 1)
        member = (id0 == (col >> 4)) | (id1 == (col >> 4))
        before = dot(ones_at(iota((32, 32), 1) < iota((32, 32), 0)), ones_at(member))
        hit = member & (before == (col & 7).astype(F32))
        side = (col >> 3) & 1
        PK[i] = jnp.concatenate([ones_at(hit & (side == 0)), ones_at(hit & (side == 1))], axis=0)
        last = member & (before == 8.0)
        PL[i] = jnp.concatenate([ones_at(last & ((col & 15) == j)) for j in range(NJ)], axis=0)

    def g_dispatch(i, k, piece):
        gate = jnp.concatenate([GT[i]] * (K // 128), axis=1)
        left = (dot(DG[i], piece(k, 0)) * gate).reshape(8, 8, K)
        right = (dot(DG[i], piece(k, 1)) * gate).reshape(8, 8, K)
        GS[i, :, :, K * k:K * k + K] = jnp.concatenate([left, right], axis=1).astype(BF)
        if k == NC - 1:
            stacked = jnp.concatenate(
                [piece(n, h)[:, 128 * m:128 * m + 128] for h in range(2) for n in range(NC) for m in range(K // 128)],
                axis=0,
            )
            GS[i, :, :, H:H + 128] = (dot(DL[i], stacked) * GL[i]).astype(BF).reshape(8, 16, 128)
        part, lanes = e // 4, to_expert[k]
        for p in peers:
            send(GS.at[i, p, :, lanes], GR.at[i, y, e, :, lanes], gx_sem.at[i, part, k], (z, p, y))
        pltpu.make_async_copy(GS.at[i, e, :, lanes], GR.at[i, y, e, :, lanes], gx_sem.at[i, part, k]).start()

    def g_first(i, k):
        lower, upper = GR.at[i, y, pl.ds(0, 4), :, to_expert[k]], GR.at[i, y, pl.ds(4, 4), :, to_expert[k]]
        arrived(lower, gx_sem.at[i, 0, k])
        send(lower, lower, ga_sem.at[i, 0, 0, k], above)
        arrived(upper, gx_sem.at[i, 1, k])
        send(upper, upper, ga_sem.at[i, 1, 1, k], below)
        send(upper, upper, ga_sem.at[i, 0, 1, k], above)
        send(lower, lower, ga_sem.at[i, 1, 0, k], below)

    def g_second(i, k):
        lower, upper = GR.at[i, yp, pl.ds(0, 4), :, to_expert[k]], GR.at[i, yn, pl.ds(4, 4), :, to_expert[k]]
        arrived(lower, ga_sem.at[i, 0, 0, k])
        send(lower, lower, gf_sem.at[i, 0, k], above)
        arrived(upper, ga_sem.at[i, 1, 1, k])
        send(upper, upper, gf_sem.at[i, 1, k], below)

    def g_finish(i, k):
        lanes = to_expert[k]
        arrived(GR.at[i, yp, pl.ds(4, 4), :, lanes], ga_sem.at[i, 0, 1, k])
        arrived(GR.at[i, yn, pl.ds(0, 4), :, lanes], ga_sem.at[i, 1, 0, k])
        arrived(GR.at[i, y2, pl.ds(0, 4), :, lanes], gf_sem.at[i, 0, k])
        arrived(GR.at[i, y2, pl.ds(4, 4), :, lanes], gf_sem.at[i, 1, k])

        @pl.loop(0, 8)
        def _(s):
            folded = GR[i, :, s, :, K * k:K * k + K].astype(F32)
            GB[i, s, :, K * k:K * k + K] = folded[:, 0:8].reshape(32, K).astype(BF)
            GB[i, s, :, H + K * k:H + K * k + K] = folded[:, 8:16].reshape(32, K).astype(BF)

        if k == NC - 1:
            tails = dot(SELG[...], GR[i, :, :, :, H:H + 128].reshape(512, 128)).astype(BF)
            for j in range(NJ):
                GB[i, 8, :, 128 * j:128 * j + 128] = tails[32 * j:32 * j + 32]

    def compute_a(i):
        c = i // 2
        preact = dot(XB[i].reshape(288, D), W1[c])
        hidden = dot(GB[i].reshape(288, D), W2[c], ((1,), (1,)))
        squash = 1.0 / (1.0 + jnp.exp(-preact))
        AC[i] = (preact * squash).astype(BF)
        grad = (hidden * (squash * (1.0 + preact * (1.0 - squash)))).astype(BF)
        PG[i] = grad

    def compute_b(i, k):
        c = i // 2
        main = PG[i, 0:256]
        left = dot(main, W1[c, K * k:K * k + K], ((1,), (1,))).reshape(8, 4, 8, K)
        right = dot(main, W1[c, H + K * k:H + K * k + K], ((1,), (1,))).reshape(8, 4, 8, K)
        for b in range(4):
            PR[i, b, :, :, 128 + K * k:128 + K * k + K] = jnp.concatenate([left[:, b], right[:, b]], axis=1).astype(BF)
        if k == 0:
            tail = dot(PG[i, 256:288], W1[c], ((1,), (1,))).astype(BF)
            stacked = jnp.concatenate([tail[:, 128 * j:128 * j + 128] for j in range(NJ)], axis=0)
            PR[i, :, :, :, 0:128] = dot(SELP[...], stacked).astype(BF).reshape(4, 8, 16, 128)
        r_first(i, k)

    def r_first(i, k):
        lanes, lower, upper = back[k], pl.ds(0, 4), pl.ds(4, 4)
        send(PR.at[i, y2, lower, :, lanes], RA.at[i, 0, :, :, lanes], r1_sem.at[i, 0, k], above)
        send(PR.at[i, y2, upper, :, lanes], RA.at[i, 1, :, :, lanes], r1_sem.at[i, 1, k], below)
        send(PR.at[i, yn, upper, :, lanes], FR.at[i, 0, upper, :, lanes], re_sem.at[i, 0, k], above)
        send(PR.at[i, yp, lower, :, lanes], FR.at[i, 1, lower, :, lanes], re_sem.at[i, 1, k], below)

    def r_second(i, k):
        lanes, lower, upper = back[k], pl.ds(0, 4), pl.ds(4, 4)
        arrived(RA.at[i, 0, :, :, lanes], r1_sem.at[i, 0, k])
        SB[i, 0, :, :, lanes] = (PR[i, yn, 0:4, :, lanes].astype(F32) + RA[i, 0, :, :, lanes].astype(F32)).astype(BF)
        send(SB.at[i, 0, :, :, lanes], FR.at[i, 0, lower, :, lanes], r2_sem.at[i, 0, k], above)
        arrived(RA.at[i, 1, :, :, lanes], r1_sem.at[i, 1, k])
        SB[i, 1, :, :, lanes] = (PR[i, yp, 4:8, :, lanes].astype(F32) + RA[i, 1, :, :, lanes].astype(F32)).astype(BF)
        send(SB.at[i, 1, :, :, lanes], FR.at[i, 1, upper, :, lanes], r2_sem.at[i, 1, k], below)

    def r_third(i, k):
        lanes, lower, upper = back[k], pl.ds(0, 4), pl.ds(4, 4)
        arrived(FR.at[i, 0, upper, :, lanes], re_sem.at[i, 0, k])
        arrived(FR.at[i, 1, lower, :, lanes], re_sem.at[i, 1, k])
        arrived(FR.at[i, 0, lower, :, lanes], r2_sem.at[i, 0, k])
        arrived(FR.at[i, 1, upper, :, lanes], r2_sem.at[i, 1, k])
        RS[i, :, :, lanes] = (
            PR[i, y, :, :, lanes].astype(F32) + FR[i, 0, :, :, lanes].astype(F32) + FR[i, 1, :, :, lanes].astype(F32)
        ).astype(BF)
        for p in peers:
            send(RS.at[i, p, :, lanes], RR.at[i, e, :, lanes], rr_sem.at[i, k], (z, p, y))
        pltpu.make_async_copy(RS.at[i, e, :, lanes], RR.at[i, e, :, lanes], rr_sem.at[i, k]).start()

    def r_fourth(i, k, piece):
        c, t = i // 2, i % 2
        arrived(RR.at[i, :, :, back[k]], rr_sem.at[i, k])
        main = dot(PK[i], RR[i, :, :, 128 + K * k:128 + K * k + K].reshape(128, K))
        per = K // 128
        for h in range(2):
            j = NJ // 2 * h + per * k
            tail = dot(PL[i, 32 * j:32 * j + 32 * per], RR[i, :, :, 0:128].reshape(128, 128))
            own = piece(k, h).astype(F32)
            for m in range(per):
                at = slice(128 * m, 128 * m + 128)
                RES[i, k, h, :, at] = (own[:, at] + (main[32 * h:32 * h + 32, at] + tail[32 * m:32 * m + 32])).astype(BF)
            OUT[i, :, H * h + K * k:H * h + K * k + K] = RES[i, k, h]
        if k == NC - 1:
            copy = pltpu.make_async_copy(OUT.at[i], out.at[2 * t + c], out_sem.at[i])
            copy.start()
            outs.append(copy)

    def grads_in(c, n, count):
        grad = PG[2 * c:2 * c + 2].reshape(576, -1)

        @pl.loop(n, n + count)
        def _(n):
            at = pl.ds(pl.multiple_of(n * 256, 256), 256)
            WG1[c, at, :] = dot(XB[2 * c:2 * c + 2, :, :, at].reshape(576, 256), grad, ((0,), (0,))).astype(BF)

        if n + count == D // 256:
            copy = pltpu.make_async_copy(WG1.at[c], gin.at[c], o_sem.at[c, 0])
            copy.start()
            outs.append(copy)

    def grads_out(c, n):
        at = pl.ds(512 * n, 512)
        act = AC[2 * c:2 * c + 2].reshape(576, -1)
        WG2[c, :, at] = dot(act, GB[2 * c:2 * c + 2, :, :, at].reshape(576, 512), ((0,), (0,))).astype(BF)
        if n == D // 512 - 1:
            copy = pltpu.make_async_copy(WG2.at[c], gout.at[c], o_sem.at[c, 1])
            copy.start()
            outs.append(copy)

    def from_flight(c):
        return lambda k, h: flight[c, :, H * h + K * k:H * h + K * k + K]

    def upper_piece(k, h):
        return jnp.where(z == 0, entering[:, H * h + K * k:H * h + K * k + K], INC[1, k, h])

    def lower_piece(k, h):
        return jnp.where(z == 7, RES[2, k, h], INC[0, k, h])

    def pass_up(k):
        send(RES.at[A, k], INC.at[1, k], z_sem.at[1, k], z_up)

    def pass_down(k):
        send(RES.at[B, k], INC.at[0, k], z_sem.at[0, k], z_down)

    def from_below(k):
        arrived(INC.at[1, k], z_sem.at[1, k])

    def from_above(k):
        arrived(INC.at[0, k], z_sem.at[0, k])

    A, B, C, E = 2, 0, 3, 1
    flight1, flight0 = from_flight(1), from_flight(0)
    each = range(NC)
    prepare(A)
    prepare(B)
    for copy in loads:
        copy.wait()
    pl.semaphore_wait(barrier, len(greeted))
    ids_send()
    x_send(A)
    x_send(B)
    for k in each:
        g_dispatch(A, k, flight1)
    for k in each:
        g_dispatch(B, k, flight0)
    ids_wait()
    x_forward(A)
    x_dispatch(A, 0)
    for k in each:
        g_first(A, k)
    x_forward(B)
    x_dispatch(A, 1)
    g_second(A, 0)
    x_send(C)
    for k in each[1:]:
        g_second(A, k)
    for k in each:
        g_first(B, k)
    x_dispatch(B, 0)
    x_dispatch(B, 1)
    prepare_return(A)
    prepare(C)
    x_forward(C)
    for copy in weights[0] + weights[1]:
        copy.wait()
    x_finish(A)
    for k in each:
        g_finish(A, k)
    compute_a(A)
    for k in each:
        compute_b(A, k)
    for k in each:
        g_second(B, k)
    r_second(A, 0)
    x_dispatch(C, 0)
    for k in each[1:]:
        r_second(A, k)
    x_send(E)
    for k in each:
        g_finish(B, k)
    x_finish(B)
    r_third(A, 0)
    compute_a(B)
    for k in each[1:]:
        r_third(A, k)
    for k in each:
        compute_b(B, k)
    for k in each:
        r_fourth(A, k, flight1)
        pass_up(k)
    x_dispatch(C, 1)
    x_forward(E)
    prepare_return(B)
    prepare(E)
    for k in each:
        r_second(B, k)
        from_below(k)
        g_dispatch(C, k, upper_piece)
    for k in each:
        r_third(B, k)
        g_first(C, k)
    x_dispatch(E, 0)
    for k in each:
        r_fourth(B, k, flight0)
        pass_down(k)
    prepare_return(C)
    prepare_return(E)
    for k in each:
        g_second(C, k)
        from_above(k)
        g_dispatch(E, k, lower_piece)
    x_dispatch(E, 1)
    x_finish(C)
    for k in each:
        g_finish(C, k)
    compute_a(C)
    for k in each:
        g_first(E, k)
        compute_b(C, k)
    grads_in(1, 0, 2)
    g_second(E, 0)
    grads_in(1, 2, 2)
    for k in each[1:]:
        g_second(E, k)
    grads_in(1, 4, 2)
    for k in each:
        r_second(C, k)
    grads_out(1, 0)
    x_finish(E)
    for k in each:
        g_finish(E, k)
    compute_a(E)
    for k in each:
        compute_b(E, k)
    for k in each:
        r_third(C, k)
    grads_out(1, 1)
    grads_out(1, 2)
    r_second(E, 0)
    grads_in(0, 0, 2)
    for k in each[1:]:
        r_second(E, k)
    for k in each:
        r_fourth(C, k, upper_piece)
    grads_in(0, 2, 4)
    for k in each:
        r_third(E, k)
        grads_out(0, k)
    grads_out(0, 2)
    for k in each:
        r_fourth(E, k, lower_piece)
    for copy in sends:
        copy.wait_send()
    for copy in outs:
        copy.wait()


def copier(a, b, c, a_out, b_out, c_out, a_held, b_held, c_held, in_sem, out_sem):
    parts = []
    for source, held, target in ((b, b_held, b_out), (c, c_held, c_out)):
        rows = source.shape[1] // 2
        for i in range(2):
            for n in range(2):
                at = (i, pl.ds(rows * n, rows))
                parts.append((source.at[at], held.at[at], target.at[at]))
    parts.append((a, a_held, a_out))
    loads = [pltpu.make_async_copy(x, v, in_sem.at[n]) for n, (x, v, _) in enumerate(parts)]
    stores = [pltpu.make_async_copy(v, w, out_sem.at[n]) for n, (_, v, w) in enumerate(parts)]
    for load in loads:
        load.start()
    for load, store in zip(loads, stores):
        load.wait()
        store.start()
    for store in stores:
        store.wait()


def per_device(in_flight, entering, checkpoints, expert_ids, gates, w_in, w_out):
    D = in_flight.shape[-1]
    F = w_in.shape[-1]
    T = 4
    W = D // 2 + 128
    K = D // 2 // NC
    ids = expert_ids[:, :, 0]
    ids_rows = ids.swapaxes(2, 3).reshape(2 * T, 32)
    gate_rows = gates[:, :, 0].swapaxes(2, 3).reshape(2 * T, 32)
    vmem, anywhere = pl.BlockSpec(memory_space=pltpu.VMEM), pl.BlockSpec(memory_space=pl.ANY)
    dma = pltpu.SemaphoreType.DMA
    out, gin, gout = pl.pallas_call(
        kernel,
        out_shape=(
            jax.ShapeDtypeStruct((T, 32, D), BF),
            jax.ShapeDtypeStruct((2, D, F), BF),
            jax.ShapeDtypeStruct((2, F, D), BF),
        ),
        in_specs=[anywhere] * 3 + [vmem] * 2 + [anywhere] * 2,
        out_specs=(anywhere, anywhere, anywhere),
        scratch_shapes=[
            pltpu.VMEM((2, 32, D), BF),
            pltpu.VMEM((32, D), BF),
            pltpu.VMEM((2, D, F), BF),
            pltpu.VMEM((2, F, D), BF),
            pltpu.VMEM((T, 4, 32, D), BF),
            pltpu.VMEM((T, 2, 8, 16, D), BF),
            pltpu.VMEM((T, 8, 16, D // 4), BF),
            pltpu.VMEM((T, 9, 32, D), BF),
            pltpu.VMEM((T, 8, 16, D // 4), BF),
            pltpu.VMEM((4, 8, 128), I32),
            pltpu.VMEM((T, 8, 16, W), BF),
            pltpu.VMEM((T, 4, 8, 16, W), BF),
            pltpu.VMEM((T, 9, 32, D), BF),
            pltpu.VMEM((T, 288, F), BF),
            pltpu.VMEM((T, 288, F), BF),
            pltpu.VMEM((T, 4, 8, 16, W), BF),
            pltpu.VMEM((T, 2, 4, 16, W), BF),
            pltpu.VMEM((T, 2, 4, 16, W), BF),
            pltpu.VMEM((T, 2, 8, 16, W), BF),
            pltpu.VMEM((T, 8, 16, W), BF),
            pltpu.VMEM((T, 8, 16, W), BF),
            pltpu.VMEM((2, NC, 2, 32, K), BF),
            pltpu.VMEM((T, NC, 2, 32, K), BF),
            pltpu.VMEM((384, 512), BF),
            pltpu.VMEM((512, 384), BF),
            pltpu.VMEM((2, D, F), BF),
            pltpu.VMEM((2, F, D), BF),
            pltpu.VMEM((8, D // 4), I32),
            pltpu.VMEM((32, 8), I32),
            pltpu.VMEM((T, 64, 32), BF),
            pltpu.VMEM((T, 64, 128), F32),
            pltpu.VMEM((T, 128, D // 4), BF),
            pltpu.VMEM((T, 128, 128), F32),
            pltpu.VMEM((T, 64, 128), BF),
            pltpu.VMEM((T, D // 4, 128), BF),
            pltpu.VMEM((T, 32, D), BF),
            dma((112 + 108 * NC,)), dma((6,)), dma((3,)),
            dma((T, 2)), dma((T, 2)), dma((T,)), dma((T,)),
            dma((T, 2, NC)), dma((T, 2, 2, NC)), dma((T, 2, NC)),
            dma((T, 2, NC)), dma((T, 2, NC)), dma((T, 2, NC)), dma((T, NC)), dma((2, NC)),
            dma((2, 2)), dma((2, 2)), dma((4,)),
        ],
        compiler_params=pltpu.CompilerParams(
            collective_id=0, has_side_effects=True, vmem_limit_bytes=60 * 2**20
        ),
    )(in_flight[:, 0], entering[0], checkpoints.reshape(T, 32, D), ids_rows, gate_rows, w_in[:, 0, 0], w_out[:, 0, 0])
    out, gin, gout = pl.pallas_call(
        copier,
        out_shape=tuple(jax.ShapeDtypeStruct(v.shape, v.dtype) for v in (out, gin, gout)),
        in_specs=[anywhere] * 3,
        out_specs=(anywhere,) * 3,
        scratch_shapes=[pltpu.VMEM(v.shape, v.dtype) for v in (out, gin, gout)] + [dma((9,)), dma((9,))],
        compiler_params=pltpu.CompilerParams(vmem_limit_bytes=60 * 2**20),
    )(out, gin, gout)
    return out.reshape(2, 2, 1, 32, D), gin[:, None, None], gout[:, None, None]


def solution(mesh):
    tokens = P(None, None, "section", ("expert", "dp"), None)
    weight_in = P(None, "section", "expert", None, "dp")
    weight_out = P(None, "section", "expert", "dp", None)
    return jax.shard_map(
        per_device,
        mesh=mesh,
        in_specs=(P(None, "section", ("expert", "dp"), None), P(None, ("expert", "dp"), None), tokens, tokens, tokens,
                  weight_in, weight_out),
        out_specs=(tokens, weight_in, weight_out),
        check_vma=False,
    )
```

```python
import jax
import jax.numpy as jnp
from jax import lax
from jax.experimental import pallas as pl
from jax.experimental.pallas import tpu as pltpu
from jax.sharding import PartitionSpec as P

MESH = pl.DeviceIdType.MESH
BF, F32, I32 = jnp.bfloat16, jnp.float32, jnp.int32
NC = 2


def iota(shape, dim):
    return lax.broadcasted_iota(I32, shape, dim)


def ones_at(cond):
    return jnp.where(cond, 1.0, 0.0).astype(BF)


def dot(a, b, dims=((1,), (0,))):
    return lax.dot_general(a, b, (dims, ((), ())), preferred_element_type=F32)


def kernel(
    flight_in, entering_in, chk, ids_own, gat, w_in, w_out,
    out, gin, gout,
    flight, entering,
    W1, W2, XT, XS, XST, XB, XTR, IDX, GS, GR, GB, PG, AC, PR, RA, SB, FR, RS, RR, INC, RES, SELG, SELP, WG1, WG2, ids, idc, DG, GT, DL, GL, PK, PL, OUT, HELD,
    send_sem, loc_sem, id_sem, xa_sem, xf_sem, xm_sem, xt_sem, gx_sem, ga_sem, gf_sem, r1_sem, re_sem, r2_sem, rr_sem, z_sem,
    w_sem, o_sem, out_sem,
):
    D = flight.shape[2]
    H = D // 2
    K = H // NC
    to_expert = [pl.ds(K * k, K + 128 * (k == NC - 1)) for k in range(NC)]
    back = [pl.ds(128 * (k > 0) + K * k, K + 128 * (k == 0)) for k in range(NC)]
    NJ = D // 128
    Q = D // 4
    z, e, y = (lax.axis_index(a) for a in ("section", "expert", "dp"))
    yn, yp, y2 = lax.rem(y + 1, 4), lax.rem(y + 3, 4), lax.rem(y + 2, 4)
    above, below, across = (z, e, yn), (z, e, yp), (z, e, y2)
    z_up, z_down = (lax.rem(z + 1, 8), e, y), (lax.rem(z + 7, 8), e, y)
    peers = [lax.rem(e + k, 8) for k in (1, 7, 2, 6, 3, 5, 4)]

    sends, outs = [], []

    def send(src, dst, sem, device):
        copy = pltpu.make_async_remote_copy(
            src_ref=src, dst_ref=dst, send_sem=send_sem.at[len(sends)], recv_sem=sem,
            device_id=device, device_id_type=MESH,
        )
        copy.start()
        sends.append(copy)

    def arrived(ref, sem):
        pltpu.make_async_copy(ref, ref, sem).wait()

    barrier = pltpu.get_barrier_semaphore()
    greeted = [(z, p, y) for p in peers] + [above, below, across, z_up, z_down]
    for device in greeted:
        pl.semaphore_signal(barrier, inc=1, device_id=device, device_id_type=MESH)

    loads = [pltpu.make_async_copy(chk.at[2 * (i % 2) + i // 2], XT.at[i, y], loc_sem.at[i]) for i in range(4)]
    loads.append(pltpu.make_async_copy(flight_in, flight, loc_sem.at[4]))
    loads.append(pltpu.make_async_copy(entering_in, entering, loc_sem.at[5]))
    for copy in loads:
        copy.start()

    weights = []
    for c in (1, 0):
        weights.append((
            pltpu.make_async_copy(w_in.at[c], W1.at[c], w_sem.at[c, 0]),
            pltpu.make_async_copy(w_out.at[c], W2.at[c], w_sem.at[c, 1]),
        ))
        for copy in weights[-1]:
            copy.start()

    narrow = ids_own[...].astype(F32).astype(BF)
    ids[...] = dot(narrow, ones_at(iota((32, 32 * NJ), 0) == (iota((32, 32 * NJ), 1) & 31))).astype(I32)
    idc[...] = dot(ones_at(iota((32, 32), 0) == iota((32, 32), 1)), narrow, ((1,), (1,))).astype(I32)
    IDX[y] = ids[:, 0:128]
    row, col = iota((384, 512), 0), iota((384, 512), 1)
    SELG[...] = ones_at(((row >> 5) == (col & 15)) & (((row >> 2) & 7) == ((col >> 4) & 7)) & ((row & 3) == (col >> 7)))
    row, col = iota((512, 384), 0), iota((512, 384), 1)
    SELP[...] = ones_at(((col >> 5) == (row & 15)) & (((col >> 2) & 7) == ((row >> 4) & 7)) & ((col & 3) == (row >> 7)))

    def ids_send():
        for n, device in enumerate((above, below, across)):
            send(IDX.at[y], IDX.at[y], id_sem.at[n], device)

    def ids_wait():
        for n, b in enumerate((yp, yn, y2)):
            arrived(IDX.at[b], id_sem.at[n])

    def x_send(i):
        send(XT.at[i, y], XT.at[i, y], xa_sem.at[i, 0], above)
        send(XT.at[i, y], XT.at[i, y], xa_sem.at[i, 1], below)

    def x_forward(i):
        arrived(XT.at[i, yp], xa_sem.at[i, 0])
        half = XT.at[i, yp, pl.ds(0, 16)]
        send(half, half, xf_sem.at[i, 0], above)
        arrived(XT.at[i, yn], xa_sem.at[i, 1])
        half = XT.at[i, yn, pl.ds(16, 16)]
        send(half, half, xf_sem.at[i, 1], below)

    def x_dispatch(i, n):
        c, t = i // 2, i % 2
        r = 2 * (2 * t + c)
        a, b = iota((128, 128), 0), iota((128, 128), 1)
        upper = ones_at(((a >> 5) == (b >> 5)) & (a < b))
        pair = y // 2 if n == 0 else 1 - y // 2
        if n:
            arrived(XT.at[i, y2, pl.ds(0, 16)], xf_sem.at[i, 0])
            arrived(XT.at[i, y2, pl.ds(16, 16)], xf_sem.at[i, 1])
        both = jnp.where(iota((8, 128), 1) < 32, IDX[2 * pair], IDX[2 * pair + 1])
        id0, id1 = both[r:r + 1, 0:64], both[r + 1:r + 2, 0:64]
        row, col = iota((128, 64), 0), iota((128, 64), 1)
        member = ((id0 == (row >> 4)) | (id1 == (row >> 4))) & (((row >> 3) & 1) == (col >> 5))
        before = dot(ones_at(member), upper[0:64, 0:64])
        hit = member & (before == (row & 7).astype(F32))
        XS[i, pair] = dot(ones_at(hit), XT[i, pl.ds(2 * pair, 2)].reshape(64, D)).astype(BF).reshape(8, 16, D)
        rows = pl.ds(pl.multiple_of(16 * pair, 16), 16)
        for p in peers:
            send(XS.at[i, pair, p], XB.at[i, e, rows], xm_sem.at[i], (z, p, y))
        pltpu.make_async_copy(XS.at[i, pair, e], XB.at[i, e, rows], xm_sem.at[i]).start()
        if n:
            tokens = XT[i].reshape(128, D)
            lane = iota((8, 128), 1) >> 5
            every = jnp.where(lane == 0, IDX[0], jnp.where(lane == 1, IDX[1], jnp.where(lane == 2, IDX[2], IDX[3])))
            id0, id1 = every[r:r + 1], every[r + 1:r + 2]
            row, col = iota((128, 128), 0), iota((128, 128), 1)
            member = ((id0 == (row >> 4)) | (id1 == (row >> 4))) & ((row & 3) == (col >> 5))
            before = dot(ones_at(member), upper)
            hit = member & (before == 8.0)
            wide = jnp.concatenate([ones_at(hit & (((row >> 2) & 3) == q)) for q in range(4)], axis=1)
            stacked = jnp.concatenate([tokens[:, Q * q:Q * q + Q] for q in range(4)], axis=0)
            XST[i] = dot(wide, stacked).astype(BF).reshape(8, 16, Q)
            for p in peers:
                send(XST.at[i, p], XTR.at[i, e], xt_sem.at[i], (z, p, y))
            pltpu.make_async_copy(XST.at[i, e], XTR.at[i, e], xt_sem.at[i]).start()

    def x_finish(i):
        arrived(XB.at[i, pl.ds(0, 8)], xm_sem.at[i])
        arrived(XTR.at[i], xt_sem.at[i])
        row, col = iota((128, 128), 0), iota((128, 128), 1)
        pick = ones_at(((row >> 5) == ((col >> 2) & 3)) & (((row >> 2) & 7) == (col >> 4)) & ((row & 3) == (col & 3)))
        rows = dot(pick, XTR[i].reshape(128, Q)).astype(BF)
        for q in range(4):
            XB[i, 8, :, Q * q:Q * q + Q] = rows[32 * q:32 * q + 32]

    def prepare(i):
        c, t = i // 2, i % 2
        r = 2 * (2 * t + c)
        id0, id1 = ids[r:r + 1, 0:32], ids[r + 1:r + 2, 0:32]
        g0, g1 = gat[r:r + 1, :], gat[r + 1:r + 2, :]
        upper = ones_at(iota((32, 32), 0) < iota((32, 32), 1))
        row = iota((64, 32), 0)
        first = id0 == (row >> 3)
        member = first | (id1 == (row >> 3))
        before = dot(ones_at(member), upper)
        hit = member & (before == (row & 7).astype(F32))
        gate = jnp.sum(jnp.where(hit, jnp.where(first, g0, g1), 0.0), axis=1, keepdims=True)
        DG[i] = ones_at(hit)
        GT[i] = jnp.broadcast_to(gate, (64, 128))
        row = iota((128, 32), 0)
        first = id0 == (row >> 4)
        member = first | (id1 == (row >> 4))
        counted = ones_at(member)
        before = dot(counted, upper)
        gate = jnp.sum(jnp.where(member & (before == 8.0), jnp.where(first, g0, g1), 0.0), axis=1, keepdims=True)
        row, col = iota((128, 32 * NJ), 0), iota((128, 32 * NJ), 1)
        wide0, wide1 = ids[r:r + 1, :], ids[r + 1:r + 2, :]
        member = (wide0 == (row >> 4)) | (wide1 == (row >> 4))
        upper = ones_at(iota((32, 32 * NJ), 0) < (iota((32, 32 * NJ), 1) & 31))
        before = dot(counted, upper)
        DL[i] = ones_at(member & (before == 8.0) & ((row & 15) == (col >> 5)))
        GL[i] = jnp.broadcast_to(gate, (128, 128))

    def prepare_return(i):
        c, t = i // 2, i % 2
        r = 2 * (2 * t + c)
        id0, id1 = idc[:, r:r + 1], idc[:, r + 1:r + 2]
        col = iota((32, 128), 1)
        member = (id0 == (col >> 4)) | (id1 == (col >> 4))
        before = dot(ones_at(iota((32, 32), 1) < iota((32, 32), 0)), ones_at(member))
        hit = member & (before == (col & 7).astype(F32))
        side = (col >> 3) & 1
        PK[i] = jnp.concatenate([ones_at(hit & (side == 0)), ones_at(hit & (side == 1))], axis=0)
        last = member & (before == 8.0)
        PL[i] = jnp.concatenate([ones_at(last & ((col & 15) == j)) for j in range(NJ)], axis=0)

    def g_dispatch(i, k, piece):
        gate = jnp.concatenate([GT[i]] * (K // 128), axis=1)
        left = (dot(DG[i], piece(k, 0)) * gate).reshape(8, 8, K)
        right = (dot(DG[i], piece(k, 1)) * gate).reshape(8, 8, K)
        GS[i, :, :, K * k:K * k + K] = jnp.concatenate([left, right], axis=1).astype(BF)
        if k == NC - 1:
            stacked = jnp.concatenate(
                [piece(n, h)[:, 128 * m:128 * m + 128] for h in range(2) for n in range(NC) for m in range(K // 128)],
                axis=0,
            )
            GS[i, :, :, H:H + 128] = (dot(DL[i], stacked) * GL[i]).astype(BF).reshape(8, 16, 128)
        part, lanes = e // 4, to_expert[k]
        for p in peers:
            send(GS.at[i, p, :, lanes], GR.at[i, y, e, :, lanes], gx_sem.at[i, part, k], (z, p, y))
        pltpu.make_async_copy(GS.at[i, e, :, lanes], GR.at[i, y, e, :, lanes], gx_sem.at[i, part, k]).start()

    def g_first(i, k):
        lower, upper = GR.at[i, y, pl.ds(0, 4), :, to_expert[k]], GR.at[i, y, pl.ds(4, 4), :, to_expert[k]]
        arrived(lower, gx_sem.at[i, 0, k])
        send(lower, lower, ga_sem.at[i, 0, 0, k], above)
        arrived(upper, gx_sem.at[i, 1, k])
        send(upper, upper, ga_sem.at[i, 1, 1, k], below)
        send(upper, upper, ga_sem.at[i, 0, 1, k], above)
        send(lower, lower, ga_sem.at[i, 1, 0, k], below)

    def g_second(i, k):
        lower, upper = GR.at[i, yp, pl.ds(0, 4), :, to_expert[k]], GR.at[i, yn, pl.ds(4, 4), :, to_expert[k]]
        arrived(lower, ga_sem.at[i, 0, 0, k])
        send(lower, lower, gf_sem.at[i, 0, k], above)
        arrived(upper, ga_sem.at[i, 1, 1, k])
        send(upper, upper, gf_sem.at[i, 1, k], below)

    def g_finish(i, k):
        lanes = to_expert[k]
        arrived(GR.at[i, yp, pl.ds(4, 4), :, lanes], ga_sem.at[i, 0, 1, k])
        arrived(GR.at[i, yn, pl.ds(0, 4), :, lanes], ga_sem.at[i, 1, 0, k])
        arrived(GR.at[i, y2, pl.ds(0, 4), :, lanes], gf_sem.at[i, 0, k])
        arrived(GR.at[i, y2, pl.ds(4, 4), :, lanes], gf_sem.at[i, 1, k])

        @pl.loop(0, 8)
        def _(s):
            folded = GR[i, :, s, :, K * k:K * k + K].astype(F32)
            GB[i, s, :, K * k:K * k + K] = folded[:, 0:8].reshape(32, K).astype(BF)
            GB[i, s, :, H + K * k:H + K * k + K] = folded[:, 8:16].reshape(32, K).astype(BF)

        if k == NC - 1:
            tails = dot(SELG[...], GR[i, :, :, :, H:H + 128].reshape(512, 128)).astype(BF)
            for j in range(NJ):
                GB[i, 8, :, 128 * j:128 * j + 128] = tails[32 * j:32 * j + 32]

    def hidden_of(i):
        return dot(GB[i].reshape(288, D), W2[i // 2], ((1,), (1,)))

    def slope_of(i):
        preact = dot(XB[i].reshape(288, D), W1[i // 2])
        squash = 1.0 / (1.0 + jnp.exp(-preact))
        AC[i] = (preact * squash).astype(BF)
        return squash * (1.0 + preact * (1.0 - squash))

    def hidden_first(i):
        HELD[i] = hidden_of(i)

    def slope_last(i):
        PG[i] = (HELD[i] * slope_of(i)).astype(BF)

    def slope_first(i):
        HELD[i] = slope_of(i)

    def hidden_last(i):
        PG[i] = (hidden_of(i) * HELD[i]).astype(BF)

    def compute_b(i, k):
        c = i // 2
        main = PG[i, 0:256]
        left = dot(main, W1[c, K * k:K * k + K], ((1,), (1,))).reshape(8, 4, 8, K)
        right = dot(main, W1[c, H + K * k:H + K * k + K], ((1,), (1,))).reshape(8, 4, 8, K)
        for b in range(4):
            PR[i, b, :, :, 128 + K * k:128 + K * k + K] = jnp.concatenate([left[:, b], right[:, b]], axis=1).astype(BF)
        if k == 0:
            tail = dot(PG[i, 256:288], W1[c], ((1,), (1,))).astype(BF)
            stacked = jnp.concatenate([tail[:, 128 * j:128 * j + 128] for j in range(NJ)], axis=0)
            PR[i, :, :, :, 0:128] = dot(SELP[...], stacked).astype(BF).reshape(4, 8, 16, 128)
        r_first(i, k)

    def r_first(i, k):
        lanes, lower, upper = back[k], pl.ds(0, 4), pl.ds(4, 4)
        send(PR.at[i, y2, lower, :, lanes], RA.at[i, 0, :, :, lanes], r1_sem.at[i, 0, k], above)
        send(PR.at[i, y2, upper, :, lanes], RA.at[i, 1, :, :, lanes], r1_sem.at[i, 1, k], below)
        send(PR.at[i, yn, upper, :, lanes], FR.at[i, 0, upper, :, lanes], re_sem.at[i, 0, k], above)
        send(PR.at[i, yp, lower, :, lanes], FR.at[i, 1, lower, :, lanes], re_sem.at[i, 1, k], below)

    def r_second(i, k):
        lanes, lower, upper = back[k], pl.ds(0, 4), pl.ds(4, 4)
        arrived(RA.at[i, 0, :, :, lanes], r1_sem.at[i, 0, k])
        SB[i, 0, :, :, lanes] = (PR[i, yn, 0:4, :, lanes].astype(F32) + RA[i, 0, :, :, lanes].astype(F32)).astype(BF)
        send(SB.at[i, 0, :, :, lanes], FR.at[i, 0, lower, :, lanes], r2_sem.at[i, 0, k], above)
        arrived(RA.at[i, 1, :, :, lanes], r1_sem.at[i, 1, k])
        SB[i, 1, :, :, lanes] = (PR[i, yp, 4:8, :, lanes].astype(F32) + RA[i, 1, :, :, lanes].astype(F32)).astype(BF)
        send(SB.at[i, 1, :, :, lanes], FR.at[i, 1, upper, :, lanes], r2_sem.at[i, 1, k], below)

    def r_third(i, k):
        lanes, lower, upper = back[k], pl.ds(0, 4), pl.ds(4, 4)
        arrived(FR.at[i, 0, upper, :, lanes], re_sem.at[i, 0, k])
        arrived(FR.at[i, 1, lower, :, lanes], re_sem.at[i, 1, k])
        arrived(FR.at[i, 0, lower, :, lanes], r2_sem.at[i, 0, k])
        arrived(FR.at[i, 1, upper, :, lanes], r2_sem.at[i, 1, k])
        RS[i, :, :, lanes] = (
            PR[i, y, :, :, lanes].astype(F32) + FR[i, 0, :, :, lanes].astype(F32) + FR[i, 1, :, :, lanes].astype(F32)
        ).astype(BF)
        for p in peers:
            send(RS.at[i, p, :, lanes], RR.at[i, e, :, lanes], rr_sem.at[i, k], (z, p, y))
        pltpu.make_async_copy(RS.at[i, e, :, lanes], RR.at[i, e, :, lanes], rr_sem.at[i, k]).start()

    def r_fourth(i, k, piece):
        c, t = i // 2, i % 2
        arrived(RR.at[i, :, :, back[k]], rr_sem.at[i, k])
        main = dot(PK[i], RR[i, :, :, 128 + K * k:128 + K * k + K].reshape(128, K))
        per = K // 128
        for h in range(2):
            j = NJ // 2 * h + per * k
            tail = dot(PL[i, 32 * j:32 * j + 32 * per], RR[i, :, :, 0:128].reshape(128, 128))
            own = piece(k, h).astype(F32)
            for m in range(per):
                at = slice(128 * m, 128 * m + 128)
                RES[i, k, h, :, at] = (own[:, at] + (main[32 * h:32 * h + 32, at] + tail[32 * m:32 * m + 32])).astype(BF)
            OUT[i, :, H * h + K * k:H * h + K * k + K] = RES[i, k, h]
        if k == NC - 1:
            copy = pltpu.make_async_copy(OUT.at[i], out.at[2 * t + c], out_sem.at[i])
            copy.start()
            outs.append(copy)

    def grads_in(c, n, count):
        grad = PG[2 * c:2 * c + 2].reshape(576, -1)

        @pl.loop(n, n + count)
        def _(n):
            at = pl.ds(pl.multiple_of(n * 256, 256), 256)
            WG1[c, at, :] = dot(XB[2 * c:2 * c + 2, :, :, at].reshape(576, 256), grad, ((0,), (0,))).astype(BF)

        if n + count == D // 256:
            copy = pltpu.make_async_copy(WG1.at[c], gin.at[c], o_sem.at[c, 0])
            copy.start()
            outs.append(copy)

    def grads_out(c, n):
        at = pl.ds(512 * n, 512)
        act = AC[2 * c:2 * c + 2].reshape(576, -1)
        WG2[c, :, at] = dot(act, GB[2 * c:2 * c + 2, :, :, at].reshape(576, 512), ((0,), (0,))).astype(BF)
        if n == D // 512 - 1:
            copy = pltpu.make_async_copy(WG2.at[c], gout.at[c], o_sem.at[c, 1])
            copy.start()
            outs.append(copy)

    def from_flight(c):
        return lambda k, h: flight[c, :, H * h + K * k:H * h + K * k + K]

    def upper_piece(k, h):
        return jnp.where(z == 0, entering[:, H * h + K * k:H * h + K * k + K], INC[1, k, h])

    def lower_piece(k, h):
        return jnp.where(z == 7, RES[2, k, h], INC[0, k, h])

    def pass_up(k):
        send(RES.at[A, k], INC.at[1, k], z_sem.at[1, k], z_up)

    def pass_down(k):
        send(RES.at[B, k], INC.at[0, k], z_sem.at[0, k], z_down)

    def from_below(k):
        arrived(INC.at[1, k], z_sem.at[1, k])

    def from_above(k):
        arrived(INC.at[0, k], z_sem.at[0, k])

    A, B, C, E = 2, 0, 3, 1
    flight1, flight0 = from_flight(1), from_flight(0)
    each = range(NC)
    prepare(A)
    prepare(B)
    for copy in loads:
        copy.wait()
    pl.semaphore_wait(barrier, len(greeted))
    ids_send()
    x_send(A)
    x_send(B)
    for k in each:
        g_dispatch(A, k, flight1)
    for k in each:
        g_dispatch(B, k, flight0)
    ids_wait()
    x_forward(A)
    x_dispatch(A, 0)
    for k in each:
        g_first(A, k)
    x_forward(B)
    x_dispatch(A, 1)
    g_second(A, 0)
    x_send(C)
    for k in each[1:]:
        g_second(A, k)
    for k in each:
        g_first(B, k)
    x_dispatch(B, 0)
    x_dispatch(B, 1)
    prepare_return(A)
    prepare(C)
    x_forward(C)
    for copy in weights[0] + weights[1]:
        copy.wait()
    for k in each:
        g_finish(A, k)
    hidden_first(A)
    x_finish(A)
    slope_last(A)
    for k in each:
        compute_b(A, k)
    for k in each:
        g_second(B, k)
    r_second(A, 0)
    x_dispatch(C, 0)
    for k in each[1:]:
        r_second(A, k)
    for k in each:
        g_finish(B, k)
    hidden_first(B)
    x_finish(B)
    r_third(A, 0)
    slope_last(B)
    for k in each[1:]:
        r_third(A, k)
    for k in each:
        compute_b(B, k)
    x_send(E)
    for k in each:
        r_fourth(A, k, flight1)
        pass_up(k)
    x_dispatch(C, 1)
    x_forward(E)
    prepare_return(B)
    prepare(E)
    for k in each:
        r_second(B, k)
        from_below(k)
        g_dispatch(C, k, upper_piece)
    for k in each:
        r_third(B, k)
        g_first(C, k)
    x_dispatch(E, 0)
    for k in each:
        r_fourth(B, k, flight0)
        pass_down(k)
    prepare_return(C)
    prepare_return(E)
    for k in each:
        g_second(C, k)
        from_above(k)
        g_dispatch(E, k, lower_piece)
    x_dispatch(E, 1)
    x_finish(C)
    slope_first(C)
    for k in each:
        g_finish(C, k)
    hidden_last(C)
    for k in each:
        g_first(E, k)
        compute_b(C, k)
    grads_in(1, 0, 2)
    g_second(E, 0)
    grads_in(1, 2, 2)
    for k in each[1:]:
        g_second(E, k)
    grads_in(1, 4, 2)
    for k in each:
        r_second(C, k)
    grads_out(1, 0)
    x_finish(E)
    slope_first(E)
    for k in each:
        g_finish(E, k)
    hidden_last(E)
    for k in each:
        compute_b(E, k)
    for k in each:
        r_third(C, k)
    grads_out(1, 1)
    grads_out(1, 2)
    r_second(E, 0)
    grads_in(0, 0, 2)
    for k in each[1:]:
        r_second(E, k)
    for k in each:
        r_fourth(C, k, upper_piece)
    grads_in(0, 2, 4)
    for k in each:
        r_third(E, k)
    for n in range(3):
        grads_out(0, n)
    for k in each:
        r_fourth(E, k, lower_piece)
    for copy in sends:
        copy.wait_send()
    for copy in outs:
        copy.wait()


def copier(a, b, c, a_out, b_out, c_out, a_held, b_held, c_held, in_sem, out_sem):
    parts = []
    for source, held, target in ((b, b_held, b_out), (c, c_held, c_out)):
        rows = source.shape[1]
        for i in range(2):
            for n in range(1):
                at = (i, pl.ds(rows * n, rows))
                parts.append((source.at[at], held.at[at], target.at[at]))
    parts.append((a, a_held, a_out))
    loads = [pltpu.make_async_copy(x, v, in_sem.at[n]) for n, (x, v, _) in enumerate(parts)]
    stores = [pltpu.make_async_copy(v, w, out_sem.at[n]) for n, (_, v, w) in enumerate(parts)]
    for load in loads:
        load.start()
    for load, store in zip(loads, stores):
        load.wait()
        store.start()
    for store in stores:
        store.wait()


def per_device(in_flight, entering, checkpoints, expert_ids, gates, w_in, w_out):
    D = in_flight.shape[-1]
    F = w_in.shape[-1]
    T = 4
    W = D // 2 + 128
    K = D // 2 // NC
    ids = expert_ids[:, :, 0]
    ids_rows = ids.swapaxes(2, 3).reshape(2 * T, 32)
    gate_rows = gates[:, :, 0].swapaxes(2, 3).reshape(2 * T, 32)
    vmem, anywhere = pl.BlockSpec(memory_space=pltpu.VMEM), pl.BlockSpec(memory_space=pl.ANY)
    dma = pltpu.SemaphoreType.DMA
    out, gin, gout = pl.pallas_call(
        kernel,
        out_shape=(
            jax.ShapeDtypeStruct((T, 32, D), BF),
            jax.ShapeDtypeStruct((2, D, F), BF),
            jax.ShapeDtypeStruct((2, F, D), BF),
        ),
        in_specs=[anywhere] * 3 + [vmem] * 2 + [anywhere] * 2,
        out_specs=(anywhere, anywhere, anywhere),
        scratch_shapes=[
            pltpu.VMEM((2, 32, D), BF),
            pltpu.VMEM((32, D), BF),
            pltpu.VMEM((2, D, F), BF),
            pltpu.VMEM((2, F, D), BF),
            pltpu.VMEM((T, 4, 32, D), BF),
            pltpu.VMEM((T, 2, 8, 16, D), BF),
            pltpu.VMEM((T, 8, 16, D // 4), BF),
            pltpu.VMEM((T, 9, 32, D), BF),
            pltpu.VMEM((T, 8, 16, D // 4), BF),
            pltpu.VMEM((4, 8, 128), I32),
            pltpu.VMEM((T, 8, 16, W), BF),
            pltpu.VMEM((T, 4, 8, 16, W), BF),
            pltpu.VMEM((T, 9, 32, D), BF),
            pltpu.VMEM((T, 288, F), BF),
            pltpu.VMEM((T, 288, F), BF),
            pltpu.VMEM((T, 4, 8, 16, W), BF),
            pltpu.VMEM((T, 2, 4, 16, W), BF),
            pltpu.VMEM((T, 2, 4, 16, W), BF),
            pltpu.VMEM((T, 2, 8, 16, W), BF),
            pltpu.VMEM((T, 8, 16, W), BF),
            pltpu.VMEM((T, 8, 16, W), BF),
            pltpu.VMEM((2, NC, 2, 32, K), BF),
            pltpu.VMEM((T, NC, 2, 32, K), BF),
            pltpu.VMEM((384, 512), BF),
            pltpu.VMEM((512, 384), BF),
            pltpu.VMEM((2, D, F), BF),
            pltpu.VMEM((2, F, D), BF),
            pltpu.VMEM((8, D // 4), I32),
            pltpu.VMEM((32, 8), I32),
            pltpu.VMEM((T, 64, 32), BF),
            pltpu.VMEM((T, 64, 128), F32),
            pltpu.VMEM((T, 128, D // 4), BF),
            pltpu.VMEM((T, 128, 128), F32),
            pltpu.VMEM((T, 64, 128), BF),
            pltpu.VMEM((T, D // 4, 128), BF),
            pltpu.VMEM((T, 32, D), BF),
            pltpu.VMEM((T, 288, F), F32),
            dma((112 + 108 * NC,)), dma((6,)), dma((3,)),
            dma((T, 2)), dma((T, 2)), dma((T,)), dma((T,)),
            dma((T, 2, NC)), dma((T, 2, 2, NC)), dma((T, 2, NC)),
            dma((T, 2, NC)), dma((T, 2, NC)), dma((T, 2, NC)), dma((T, NC)), dma((2, NC)),
            dma((2, 2)), dma((2, 2)), dma((4,)),
        ],
        compiler_params=pltpu.CompilerParams(
            collective_id=0, has_side_effects=True, vmem_limit_bytes=60 * 2**20
        ),
    )(in_flight[:, 0], entering[0], checkpoints.reshape(T, 32, D), ids_rows, gate_rows, w_in[:, 0, 0], w_out[:, 0, 0])
    out, gin, gout = pl.pallas_call(
        copier,
        out_shape=tuple(jax.ShapeDtypeStruct(v.shape, v.dtype) for v in (out, gin, gout)),
        in_specs=[anywhere] * 3,
        out_specs=(anywhere,) * 3,
        scratch_shapes=[pltpu.VMEM(v.shape, v.dtype) for v in (out, gin, gout)] + [dma((5,)), dma((5,))],
        compiler_params=pltpu.CompilerParams(vmem_limit_bytes=60 * 2**20),
    )(out, gin, gout)
    return out.reshape(2, 2, 1, 32, D), gin[:, None, None], gout[:, None, None]


def solution(mesh):
    tokens = P(None, None, "section", ("expert", "dp"), None)
    weight_in = P(None, "section", "expert", None, "dp")
    weight_out = P(None, "section", "expert", "dp", None)
    return jax.shard_map(
        per_device,
        mesh=mesh,
        in_specs=(P(None, "section", ("expert", "dp"), None), P(None, ("expert", "dp"), None), tokens, tokens, tokens,
                  weight_in, weight_out),
        out_specs=(tokens, weight_in, weight_out),
        check_vma=False,
    )
```
